32 devices in a mesh: fsdp: 4 (over x, core), ctx: 8 (over z, y).
Axes of the slice: x: 2, y: 2, z: 4, core: 2. Of those that a mesh axis runs over, the one named last changes fastest.
Arguments:
- queries: bfloat16 [4, 1024, 2048], P('fsdp', 'ctx'), may hold values from -200 to 200
- keyvals: bfloat16 [4, 1024, 2, 512], P('fsdp', 'ctx'), may hold values from -6 to 6
- span_ids: int32 [4, 16], P('fsdp'), may hold values from 0 to 15, as said below
Outputs:
- attended: bfloat16 [4, 1024, 2048], P('fsdp', 'ctx')
The draws below stay inside these ranges and needn't reach their ends.
Inputs may be any that keep to these rules, and one draw needn't show every extreme that they name: `span_ids`: in each sequence, ctx device d holds storage spans 2d and 2d+1; storage span 2d has position span p with p < 8 and storage span 2d+1 has position span 16 - 1-p; each p belongs to exactly one device.
All inputs are finite; a program needn't handle non-finite values.
Results may differ from the reference program's by a relative error of at most 0.0041.
Values may be sent and summed in bfloat16 or wider, within the bound.
No kernel may reach another device: no remote copies, remote signals or barrier semaphores. Data moves between devices by JAX's collectives and lax.ppermute only.
A program may use at most 64 MiB of HBM per device.

```python
import math
import jax
import jax.numpy as jnp
from jax import lax

KV_HEADS = 4
GROUP = 4
HEAD_DIM = 128
SPAN = 64
SPANS = 16
SEQ = 1024
SEQS = 4


def shared_keyvals(key):
    base = jax.random.fold_in(key, 11)
    values = jax.random.normal(base, (SEQS, SEQ, 2, KV_HEADS * HEAD_DIM), jnp.float32)
    return jnp.clip(values, -6.0, 6.0)


def draw_keyvals(key, part):
    return shared_keyvals(key).astype(jnp.bfloat16)


def draw_queries(key, part):
    base = jax.random.fold_in(key, 23)
    width = KV_HEADS * GROUP * HEAD_DIM
    drawn = jax.random.normal(base, (SEQS, SEQ, width), jnp.float32)
    return jnp.clip(drawn, -200.0, 200.0).astype(jnp.bfloat16)


def draw_span_ids(key, part):
    half_count = SPANS // 2
    keys = jax.random.split(jax.random.fold_in(key, 37), SEQS)
    orders = jax.vmap(lambda one_key: jax.random.permutation(one_key, half_count))(keys).astype(jnp.int32)
    mirrored = (SPANS - 1 - orders).astype(jnp.int32)
    return jnp.stack([orders, mirrored], axis=-1).reshape(SEQS, SPANS).astype(jnp.int32)


def setup_inputs(seed: int = 0) -> dict:
    seeds = jax.random.split(jax.random.key(seed), 4)
    return {
        "queries": draw_queries(jax.random.fold_in(seeds[3], 71), 0),
        "keyvals": draw_keyvals(jax.random.fold_in(seeds[3], 71), 0),
        "span_ids": draw_span_ids(jax.random.fold_in(seeds[3], 71), 0),
    }


def attend(query_seq, keyval_seq, span_table):
    offsets = jnp.arange(SPAN, dtype=jnp.int32)
    positions = (span_table[:, None] * SPAN + offsets[None, :]).reshape(-1).astype(jnp.int32)
    keys = keyval_seq[:, 0].reshape(SEQ, KV_HEADS, HEAD_DIM).astype(jnp.float32)
    values = keyval_seq[:, 1].reshape(SEQ, KV_HEADS, HEAD_DIM).astype(jnp.float32)
    block_rows = math.gcd(SEQ, 512)
    block_count = SEQ // block_rows
    query_blocks = query_seq.reshape(block_count, block_rows, KV_HEADS, GROUP, HEAD_DIM)
    pos_blocks = positions.reshape(block_count, block_rows)
    scale = 1.0 / math.sqrt(HEAD_DIM)

    def one_block(pair):
        query_block, query_pos = pair
        scores = jnp.einsum('qhgd,khd->hgqk', query_block.astype(jnp.float32), keys) * scale
        allowed = positions[None, None, None, :] <= query_pos[None, None, :, None]
        scores = jnp.where(allowed, scores, -1e+30)
        highest = lax.optimization_barrier(jnp.max(scores, axis=-1, keepdims=True))
        weights = jnp.where(allowed, jnp.exp(scores - highest), 0.0)
        total = lax.optimization_barrier(jnp.sum(weights, axis=-1))
        rounded = weights.astype(jnp.bfloat16).astype(jnp.float32)
        summed = jnp.einsum('hgqk,khd->qhgd', rounded, values)
        result = summed / jnp.transpose(total, (2, 0, 1))[..., None]
        return result.reshape(block_rows, KV_HEADS * GROUP * HEAD_DIM).astype(jnp.bfloat16)
    outputs = lax.map(one_block, (query_blocks, pos_blocks))
    return outputs.reshape(SEQ, KV_HEADS * GROUP * HEAD_DIM)

def reference(queries, keyvals, span_ids):
    attended = lax.map(lambda triple: attend(triple[0], triple[1], triple[2]), (queries, keyvals, span_ids))
    return attended
```

```python
import functools
import math

import jax
import jax.numpy as jnp
from jax import lax
from jax.experimental import pallas as pl
from jax.experimental.pallas import tpu as pltpu
from jax.sharding import PartitionSpec as P

KV_HEADS = 4
GROUP = 4
HEAD_DIM = 128
NT = (((1,), (1,)), ((), ()))
TN = (((0,), (0,)), ((), ()))


def ring_order(count):
    return [i for i in range(count) if i % 2 == 0] + [i for i in reversed(range(count)) if i % 2]


def ring_member(place, count):
    half = (count + 1) // 2
    return jnp.where(place < half, 2 * place, 2 * (count - 1 - place) + 1)


def ring_place(member, count):
    return jnp.where(member % 2 == 0, member // 2, count - 1 - member // 2)


def attend(count, shifts, span_ref, q_ref, *refs):
    own_early, own_late = refs[0], refs[1]
    chunk_refs = refs[2 : 2 + 2 * len(shifts)]
    out_ref, q_scr, acc, top, total = refs[2 + 2 * len(shifts) :]
    rows = own_early.shape[0]
    width = KV_HEADS * HEAD_DIM
    slot_rows = GROUP * rows
    scale = math.log2(math.e) / math.sqrt(HEAD_DIM)
    me = lax.axis_index("ctx")
    place = ring_place(me, count)
    own_span = span_ref[0, 2 * me]

    for slot in range(2):
        for j in range(KV_HEADS):
            for g in range(GROUP):
                h = j * GROUP + g
                q_scr[slot, j, g * rows : (g + 1) * rows, :] = q_ref[
                    slot * rows : (slot + 1) * rows, h * HEAD_DIM : (h + 1) * HEAD_DIM
                ]

    def key(piece, j):
        return piece[:, j * HEAD_DIM : (j + 1) * HEAD_DIM]

    def value(piece, j):
        return piece[:, width + j * HEAD_DIM : width + (j + 1) * HEAD_DIM]

    def scores(k, q):
        return lax.dot_general(k, q, NT, preferred_element_type=jnp.float32) * scale

    def first(slot, j, s, v):
        new = jnp.max(s, axis=0, keepdims=True)
        p = jnp.exp2(s - new)
        top[slot, j] = new
        total[slot, j] = jnp.sum(p, axis=0, keepdims=True)
        acc[slot, j] = lax.dot_general(
            v, p.astype(jnp.bfloat16), TN, preferred_element_type=jnp.float32
        )

    def later(slot, j, s, v):
        old = top[slot, j]
        new = jnp.maximum(old, jnp.max(s, axis=0, keepdims=True))
        shrink = jnp.exp2(old - new)
        p = jnp.exp2(s - new)
        top[slot, j] = new
        total[slot, j] = total[slot, j] * shrink + jnp.sum(p, axis=0, keepdims=True)
        acc[slot, j] = acc[slot, j] * shrink + lax.dot_general(
            v, p.astype(jnp.bfloat16), TN, preferred_element_type=jnp.float32
        )

    key_row = lax.broadcasted_iota(jnp.int32, (rows, slot_rows), 0)
    query_row = lax.broadcasted_iota(jnp.int32, (rows, slot_rows), 1) % rows
    causal = key_row <= query_row
    early, late = own_early[...], own_late[...]
    for j in range(KV_HEADS):
        s = jnp.where(causal, scores(key(early, j), q_scr[0, j]), -1e30)
        first(0, j, s, value(early, j))
        s = jnp.where(causal, scores(key(late, j), q_scr[1, j]), -1e30)
        s = jnp.concatenate([scores(key(early, j), q_scr[1, j]), s], axis=0)
        first(1, j, s, jnp.concatenate([value(early, j), value(late, j)], axis=0))

    for i, shift in enumerate(shifts):
        other = ring_member((place + shift + count) % count, count)
        before = span_ref[0, 2 * other] < own_span
        slot = jnp.where(before, 0, 1)
        early, late = chunk_refs[2 * i][...], chunk_refs[2 * i + 1][...]
        picked = jnp.where(before, early, late)
        for j in range(KV_HEADS):
            later(1, j, scores(key(early, j), q_scr[1, j]), value(early, j))
        for j in range(KV_HEADS):
            later(slot, j, scores(key(picked, j), q_scr[slot, j]), value(picked, j))

    for slot in range(2):
        for j in range(KV_HEADS):
            result = (acc[slot, j] / total[slot, j]).T.astype(jnp.bfloat16)
            for g in range(GROUP):
                h = j * GROUP + g
                out_ref[
                    slot * rows : (slot + 1) * rows, h * HEAD_DIM : (h + 1) * HEAD_DIM
                ] = result[g * rows : (g + 1) * rows]


def per_device(queries, keyvals, span_ids):
    count = lax.axis_size("ctx")
    tok_rows = queries.shape[1]
    rows = tok_rows // 2
    features = queries.shape[2]
    kv_width = 2 * KV_HEADS * HEAD_DIM
    order = ring_order(count)
    ahead = [(order[i], order[(i + 1) % count]) for i in range(count)]
    back = [(b, a) for a, b in ahead]

    own = [keyvals[0, s * rows : (s + 1) * rows].reshape(rows, kv_width) for s in range(2)]
    shifts, chunks = [], []
    up, down = own, own
    for step in range(1, (count - 1) // 2 + 1):
        up = [lax.ppermute(up[0], "ctx", ahead), lax.ppermute(up[1], "ctx", ahead)]
        down = [lax.ppermute(down[0], "ctx", back), lax.ppermute(down[1], "ctx", back)]
        chunks += [up, down]
        shifts += [-step, step]
    if count % 2 == 0 and count > 1:
        chunks.append([lax.ppermute(up[0], "ctx", ahead), lax.ppermute(down[1], "ctx", back)])
        shifts.append(-(count // 2))
    pieces = own + [piece for chunk in chunks for piece in chunk]
    vmem = pl.BlockSpec(memory_space=pltpu.VMEM)
    slot_rows = GROUP * rows
    out = pl.pallas_call(
        functools.partial(attend, count, tuple(shifts)),
        out_shape=jax.ShapeDtypeStruct((tok_rows, features), jnp.bfloat16),
        in_specs=[pl.BlockSpec(memory_space=pltpu.SMEM), vmem] + [vmem] * len(pieces),
        out_specs=vmem,
        scratch_shapes=[
            pltpu.VMEM((2, KV_HEADS, slot_rows, HEAD_DIM), jnp.bfloat16),
            pltpu.VMEM((2, KV_HEADS, HEAD_DIM, slot_rows), jnp.float32),
            pltpu.VMEM((2, KV_HEADS, 1, slot_rows), jnp.float32),
            pltpu.VMEM((2, KV_HEADS, 1, slot_rows), jnp.float32),
        ],
        compiler_params=pltpu.CompilerParams(vmem_limit_bytes=48 * 1024 * 1024),
    )(span_ids, queries[0], *pieces)
    return out[None]


def solution(mesh):
    in_specs = (P("fsdp", "ctx", None), P("fsdp", "ctx", None, None), P("fsdp", None))
    out_specs = P("fsdp", "ctx", None)
    return jax.shard_map(
        per_device, mesh=mesh, in_specs=in_specs, out_specs=out_specs, check_vma=False
    )
```

```python
import functools
import math

import jax
import jax.numpy as jnp
from jax import lax
from jax.experimental import pallas as pl
from jax.experimental.pallas import tpu as pltpu
from jax.sharding import PartitionSpec as P

KV_HEADS = 4
GROUP = 4
HEAD_DIM = 128
WIDTH = KV_HEADS * HEAD_DIM
NT = (((1,), (1,)), ((), ()))
TN = (((0,), (0,)), ((), ()))


def ring_order(count):
    return [i for i in range(count) if i % 2 == 0] + [i for i in reversed(range(count)) if i % 2]


def ring_member(place, count):
    half = (count + 1) // 2
    return jnp.where(place < half, 2 * place, 2 * (count - 1 - place) + 1)


def ring_place(member, count):
    return jnp.where(member % 2 == 0, member // 2, count - 1 - member // 2)


def key(piece, j):
    return piece[:, j * HEAD_DIM : (j + 1) * HEAD_DIM]


def value(piece, j):
    return piece[:, WIDTH + j * HEAD_DIM : WIDTH + (j + 1) * HEAD_DIM]


def attend(count, shifts, begin, end, span_ref, q_ref, *refs):
    refs = list(refs)
    chunks = [(refs.pop(0), refs.pop(0)) for _ in range(len(shifts) + begin)]
    if not begin:
        top_in, total_in, acc_in = refs.pop(0), refs.pop(0), refs.pop(0)
    if end:
        out_ref = refs.pop(0)
    else:
        top_out, total_out, acc_out = refs
    rows = chunks[0][0].shape[0]
    slot_rows = GROUP * rows
    scale = math.log2(math.e) / math.sqrt(HEAD_DIM)
    me = lax.axis_index("ctx")
    place = ring_place(me, count)
    table = span_ref[...].astype(jnp.float32)
    lane = lax.broadcasted_iota(jnp.int32, table.shape, 1)

    def span_of(member):
        return jnp.sum(jnp.where(lane == 2 * member, table, 0.0))


    def queries(slot, j):
        start = slot * rows if isinstance(slot, int) else pl.multiple_of(slot * rows, rows)
        return jnp.concatenate(
            [
                q_ref[pl.ds(start, rows), (j * GROUP + g) * HEAD_DIM : (j * GROUP + g + 1) * HEAD_DIM]
                for g in range(GROUP)
            ],
            axis=0,
        )

    def weigh(v, p):
        return lax.dot_general(v, p, TN, preferred_element_type=jnp.float32)

    def scores(k, q):
        return lax.dot_general(k, q, NT, preferred_element_type=jnp.float32) * scale

    heads = range(KV_HEADS)
    result = {}
    if begin:
        early, late = chunks.pop(0)
        key_row = lax.broadcasted_iota(jnp.int32, (rows, slot_rows), 0)
        query_row = lax.broadcasted_iota(jnp.int32, (rows, slot_rows), 1) % rows
        causal = key_row <= query_row
        for j in heads:
            q = queries(0, j)
            s = jnp.where(causal, scores(key(early, j), q), -1e30)
            new = jnp.max(s, axis=0, keepdims=True)
            p = jnp.exp2(s - new)
            result[0, j] = new, jnp.sum(p, axis=0, keepdims=True), weigh(value(early, j), p.astype(jnp.bfloat16))
            q = queries(1, j)
            k = jnp.concatenate([key(early, j), key(late, j)], axis=0)
            v = jnp.concatenate([value(early, j), value(late, j)], axis=0)
            s = scores(k, q)
            s = jnp.concatenate([s[:rows], jnp.where(causal, s[rows:], -1e30)], axis=0)
            new = jnp.max(s, axis=0, keepdims=True)
            p = jnp.exp2(s - new)
            result[1, j] = new, jnp.sum(p, axis=0, keepdims=True), weigh(v, p.astype(jnp.bfloat16))
    else:
        own_span = span_of(me)
        befores, slots, picked = [], [], []
        for shift, (early, late) in zip(shifts, chunks):
            other = ring_member((place + shift + count) % count, count)
            befores.append(span_of(other) < own_span)
            slots.append(jnp.where(befores[-1], 0, 1))
            picked.append(jnp.where(befores[-1], early[...], late[...]))
        n = len(shifts)
        full, part = {}, {}
        for j in heads:
            k = jnp.concatenate([key(early, j) for early, _ in chunks], axis=0)
            full[j] = scores(k, queries(1, j))
            part[j] = [scores(key(picked[i], j), queries(slots[i], j)) for i in range(n)]
        for j in heads:
            old = [top_in[0, j], top_in[1, j]]
            most = [jnp.max(s, axis=0, keepdims=True) for s in part[j]]
            new = [old[0], jnp.maximum(old[1], jnp.max(full[j], axis=0, keepdims=True))]
            for i in range(n):
                new[0] = jnp.maximum(new[0], jnp.where(befores[i], most[i], -1e30))
                new[1] = jnp.maximum(new[1], jnp.where(befores[i], -1e30, most[i]))
            p = jnp.exp2(full[j] - new[1])
            shrink = [jnp.exp2(old[slot] - new[slot]) for slot in range(2)]
            added = [total_in[0, j] * shrink[0], total_in[1, j] * shrink[1] + jnp.sum(p, axis=0, keepdims=True)]
            weights = [[], [p.astype(jnp.bfloat16)]]
            values = [[value(picked[i], j) for i in range(n)], [value(early, j) for early, _ in chunks]]
            values[1] += values[0]
            for i in range(n):
                p = jnp.exp2(part[j][i] - jnp.where(befores[i], new[0], new[1]))
                t = jnp.sum(p, axis=0, keepdims=True)
                p = p.astype(jnp.bfloat16)
                zero = jnp.zeros_like(p)
                added[0] = added[0] + jnp.where(befores[i], t, 0.0)
                added[1] = added[1] + jnp.where(befores[i], 0.0, t)
                weights[0].append(jnp.where(befores[i], p, zero))
                weights[1].append(jnp.where(befores[i], zero, p))
            for slot in range(2):
                update = weigh(
                    jnp.concatenate(values[slot], axis=0), jnp.concatenate(weights[slot], axis=0)
                )
                result[slot, j] = new[slot], added[slot], acc_in[slot, j] * shrink[slot] + update

    for (slot, j), (new, added, update) in result.items():
        if end:
            done = (update * (1.0 / added)).astype(jnp.bfloat16).T
            for g in range(GROUP):
                h = j * GROUP + g
                out_ref[
                    slot * rows : (slot + 1) * rows, h * HEAD_DIM : (h + 1) * HEAD_DIM
                ] = done[g * rows : (g + 1) * rows]
        else:
            top_out[slot, j] = new
            total_out[slot, j] = added
            acc_out[slot, j] = update


def fold(count, shifts, pieces, state, end, span_ids, queries):
    vmem = pl.BlockSpec(memory_space=pltpu.VMEM)
    tok_rows, features = queries.shape
    slot_rows = GROUP * (tok_rows // 2)
    begin = state is None
    state = [] if begin else list(state)
    if end:
        out_shape = jax.ShapeDtypeStruct((tok_rows, features), jnp.bfloat16)
    else:
        row = jax.ShapeDtypeStruct((2, KV_HEADS, 1, slot_rows), jnp.float32)
        out_shape = [row, row, jax.ShapeDtypeStruct((2, KV_HEADS, HEAD_DIM, slot_rows), jnp.float32)]
    keys = (len(pieces) // 2) * tok_rows
    return pl.pallas_call(
        functools.partial(attend, count, tuple(shifts), begin, end),
        out_shape=out_shape,
        in_specs=[vmem] * (2 + len(pieces) + len(state)),
        out_specs=vmem if end else [vmem] * 3,
        compiler_params=pltpu.CompilerParams(vmem_limit_bytes=32 * 1024 * 1024),
        cost_estimate=pl.CostEstimate(
            flops=2 * keys * features * tok_rows,
            bytes_accessed=2 * keys * 2 * WIDTH + 4 * tok_rows * features,
            transcendentals=keys * tok_rows * KV_HEADS * GROUP // 2,
        ),
    )(span_ids, queries, *pieces, *state)


def per_device(queries, keyvals, span_ids):
    count = lax.axis_size("ctx")
    rows = queries.shape[1] // 2
    order = ring_order(count)
    ahead = [(order[i], order[(i + 1) % count]) for i in range(count)]
    back = [(b, a) for a, b in ahead]

    flat = lax.optimization_barrier(keyvals[0].reshape(2 * rows, 2 * WIDTH))
    own = [flat[:rows], flat[rows:]]
    up, down = own, own
    last = count // 2
    held, state = ([], own), None
    for step in range(1, last + 1):
        if step > 1:
            state = fold(count, *held, state, False, span_ids, queries[0])
            up[0], *state = lax.optimization_barrier((up[0], *state))
            held = shifts, pieces
        if 2 * step < count:
            up = [lax.ppermute(piece, "ctx", ahead) for piece in up]
            down = [lax.ppermute(piece, "ctx", back) for piece in down]
            shifts, pieces = [-step, step], up + down
        else:
            shifts = [-step]
            pieces = [lax.ppermute(up[0], "ctx", ahead), lax.ppermute(down[1], "ctx", back)]
    if last:
        state = fold(count, *held, state, False, span_ids, queries[0])
        held = shifts, pieces
    return fold(count, *held, state, True, span_ids, queries[0])[None]


def solution(mesh):
    in_specs = (P("fsdp", "ctx", None), P("fsdp", "ctx", None, None), P("fsdp", None))
    out_specs = P("fsdp", "ctx", None)
    return jax.shard_map(
        per_device, mesh=mesh, in_specs=in_specs, out_specs=out_specs, check_vma=False
    )
```

```python
import functools
import math

import jax
import jax.numpy as jnp
from jax import lax
from jax.experimental import pallas as pl
from jax.experimental.pallas import tpu as pltpu
from jax.sharding import PartitionSpec as P

KV_HEADS = 4
GROUP = 4
HEAD_DIM = 128
WIDTH = KV_HEADS * HEAD_DIM
NT = (((1,), (1,)), ((), ()))
TN = (((0,), (0,)), ((), ()))


def ring_order(count):
    return [i for i in range(count) if i % 2 == 0] + [i for i in reversed(range(count)) if i % 2]


def ring_member(place, count):
    half = (count + 1) // 2
    return jnp.where(place < half, 2 * place, 2 * (count - 1 - place) + 1)


def ring_place(member, count):
    return jnp.where(member % 2 == 0, member // 2, count - 1 - member // 2)


def key(piece, j):
    return piece[:, j * HEAD_DIM : (j + 1) * HEAD_DIM]


def value(piece, j):
    return piece[:, WIDTH + j * HEAD_DIM : WIDTH + (j + 1) * HEAD_DIM]


def read_queries(q_ref, slot, rows, j):
    start = slot * rows if isinstance(slot, int) else pl.multiple_of(slot * rows, rows)
    return jnp.concatenate(
        [
            q_ref[pl.ds(start, rows), (j * GROUP + g) * HEAD_DIM : (j * GROUP + g + 1) * HEAD_DIM]
            for g in range(GROUP)
        ],
        axis=0,
    )


def scores(k, q):
    scale = math.log2(math.e) / math.sqrt(HEAD_DIM)
    return lax.dot_general(k, q, NT, preferred_element_type=jnp.float32) * scale


def weigh(v, p):
    return lax.dot_general(v, p, TN, preferred_element_type=jnp.float32)


def comes_before(count, shifts, span_ref):
    place = ring_place(lax.axis_index("ctx"), count)
    table = span_ref[...].astype(jnp.float32)
    lane = lax.broadcasted_iota(jnp.int32, table.shape, 1)

    def span_of(shift):
        member = ring_member((place + shift + count) % count, count)
        return jnp.sum(jnp.where(lane == 2 * member, table, 0.0))

    own_span = span_of(0)
    return [span_of(shift) < own_span for shift in shifts]


def normalized(total, acc):
    return (acc * (1.0 / total)).astype(jnp.bfloat16).T


def attend(count, shifts, begin, end, span_ref, q_ref, *refs):
    refs = list(refs)
    chunks = [(refs.pop(0), refs.pop(0)) for _ in range(len(shifts) + begin)]
    if not begin:
        top_in, total_in, acc_in = refs.pop(0), refs.pop(0), refs.pop(0)
    if end:
        out_ref = refs.pop(0)
    else:
        top_out, total_out, acc_out = refs
    rows = chunks[0][0].shape[0]
    slot_rows = GROUP * rows

    def queries(slot, j):
        return read_queries(q_ref, slot, rows, j)

    heads = range(KV_HEADS)
    result = {}
    if begin:
        early, late = chunks.pop(0)
        key_row = lax.broadcasted_iota(jnp.int32, (rows, slot_rows), 0)
        query_row = lax.broadcasted_iota(jnp.int32, (rows, slot_rows), 1) % rows
        causal = key_row <= query_row
        for j in heads:
            q = queries(0, j)
            s = jnp.where(causal, scores(key(early, j), q), -1e30)
            new = jnp.max(s, axis=0, keepdims=True)
            p = jnp.exp2(s - new)
            result[0, j] = new, jnp.sum(p, axis=0, keepdims=True), weigh(value(early, j), p.astype(jnp.bfloat16))
            q = queries(1, j)
            k = jnp.concatenate([key(early, j), key(late, j)], axis=0)
            v = jnp.concatenate([value(early, j), value(late, j)], axis=0)
            s = scores(k, q)
            s = jnp.concatenate([s[:rows], jnp.where(causal, s[rows:], -1e30)], axis=0)
            new = jnp.max(s, axis=0, keepdims=True)
            p = jnp.exp2(s - new)
            result[1, j] = new, jnp.sum(p, axis=0, keepdims=True), weigh(v, p.astype(jnp.bfloat16))
    else:
        n = len(shifts)
        befores = comes_before(count, shifts, span_ref)
        slots = [jnp.where(before, 0, 1) for before in befores]
        picked = [
            jnp.where(before, early[...], late[...]) for before, (early, late) in zip(befores, chunks)
        ]
        full, part = {}, {}
        for j in heads:
            k = jnp.concatenate([key(early, j) for early, _ in chunks], axis=0)
            full[j] = scores(k, queries(1, j))
            part[j] = [scores(key(picked[i], j), queries(slots[i], j)) for i in range(n)]
        for j in heads:
            old = [top_in[0, j], top_in[1, j]]
            most = [jnp.max(s, axis=0, keepdims=True) for s in part[j]]
            new = [old[0], jnp.maximum(old[1], jnp.max(full[j], axis=0, keepdims=True))]
            for i in range(n):
                new[0] = jnp.maximum(new[0], jnp.where(befores[i], most[i], -1e30))
                new[1] = jnp.maximum(new[1], jnp.where(befores[i], -1e30, most[i]))
            p = jnp.exp2(full[j] - new[1])
            shrink = [jnp.exp2(old[slot] - new[slot]) for slot in range(2)]
            added = [total_in[0, j] * shrink[0], total_in[1, j] * shrink[1] + jnp.sum(p, axis=0, keepdims=True)]
            weights = [[], [p.astype(jnp.bfloat16)]]
            values = [[value(picked[i], j) for i in range(n)], [value(early, j) for early, _ in chunks]]
            values[1] += values[0]
            for i in range(n):
                p = jnp.exp2(part[j][i] - jnp.where(befores[i], new[0], new[1]))
                t = jnp.sum(p, axis=0, keepdims=True)
                p = p.astype(jnp.bfloat16)
                zero = jnp.zeros_like(p)
                added[0] = added[0] + jnp.where(befores[i], t, 0.0)
                added[1] = added[1] + jnp.where(befores[i], 0.0, t)
                weights[0].append(jnp.where(befores[i], p, zero))
                weights[1].append(jnp.where(befores[i], zero, p))
            for slot in range(2):
                update = weigh(
                    jnp.concatenate(values[slot], axis=0), jnp.concatenate(weights[slot], axis=0)
                )
                result[slot, j] = new[slot], added[slot], acc_in[slot, j] * shrink[slot] + update

    for (slot, j), (new, added, update) in result.items():
        if end:
            done = normalized(added, update)
            for g in range(GROUP):
                h = j * GROUP + g
                out_ref[
                    slot * rows : (slot + 1) * rows, h * HEAD_DIM : (h + 1) * HEAD_DIM
                ] = done[g * rows : (g + 1) * rows]
        else:
            top_out[slot, j] = new
            total_out[slot, j] = added
            acc_out[slot, j] = update


def fold_heads(old, piece, queries, counts):
    heads = range(KV_HEADS)
    s = [scores(key(piece, j), queries[j]) for j in heads]
    most = [jnp.max(s[j], axis=0, keepdims=True) for j in heads]
    if counts is not None:
        most = [jnp.where(counts, most[j], -1e30) for j in heads]
    new = [jnp.maximum(old[j][0], most[j]) for j in heads]
    if counts is not None:
        s = [jnp.where(counts, s[j], -1e30) for j in heads]
    p = [jnp.exp2(s[j] - new[j]) for j in heads]
    update = [weigh(value(piece, j), p[j].astype(jnp.bfloat16)) for j in heads]
    shrink = [jnp.exp2(old[j][0] - new[j]) for j in heads]
    total = [old[j][1] * shrink[j] + jnp.sum(p[j], axis=0, keepdims=True) for j in heads]
    acc = [old[j][2] * shrink[j] + update[j] for j in heads]
    return list(zip(new, total, acc))


def finish(count, shift, slot, span_ref, q_ref, piece, *refs):
    refs = list(refs)
    top_in, total_in, acc_in = refs.pop(0), refs.pop(0), refs.pop(0)
    if slot:
        refs.pop(0)
        out_ref, done, sems = refs
    else:
        out_ref, top_out, total_out, acc_out, done, sems = refs
    rows = piece.shape[0]
    (before,) = comes_before(count, [shift], span_ref)

    def folded(i, counts):
        old = [(top_in[i, j], total_in[i, j], acc_in[i, j]) for j in range(KV_HEADS)]
        queries = [read_queries(q_ref, i, rows, j) for j in range(KV_HEADS)]
        return fold_heads(old, piece, queries, counts)

    states = folded(slot, jnp.logical_not(before) if slot else before)
    copies = []
    for j in range(KV_HEADS):
        _, total, acc = states[j]
        result = normalized(total, acc)
        for g in range(GROUP):
            h = j * GROUP + g
            done[:, h * HEAD_DIM : (h + 1) * HEAD_DIM] = result[g * rows : (g + 1) * rows]
        columns = slice(j * GROUP * HEAD_DIM, (j + 1) * GROUP * HEAD_DIM)
        copies.append(
            pltpu.make_async_copy(
                done.at[:, columns], out_ref.at[slot * rows : (slot + 1) * rows, columns], sems.at[j]
            )
        )
        copies[-1].start()
    if not slot:
        states = folded(1, None)
        for j in range(KV_HEADS):
            top_out[1, j], total_out[1, j], acc_out[1, j] = states[j]
    for copy in copies:
        copy.wait()


def end(count, shift, slot, piece, state, out, span_ids, queries):
    tok_rows, features = queries.shape
    rows = tok_rows // 2
    vmem, hbm = pl.BlockSpec(memory_space=pltpu.VMEM), pl.BlockSpec(memory_space=pltpu.HBM)
    result = jax.ShapeDtypeStruct((tok_rows, features), queries.dtype)
    like = [jax.ShapeDtypeStruct(part.shape, part.dtype) for part in state]
    return pl.pallas_call(
        functools.partial(finish, count, shift, slot),
        out_shape=result if slot else [result, *like],
        in_specs=[vmem] * 6 + [hbm] * slot,
        out_specs=hbm if slot else [hbm] + [vmem] * 3,
        scratch_shapes=[
            pltpu.VMEM((rows, features), queries.dtype),
            pltpu.SemaphoreType.DMA((KV_HEADS,)),
        ],
        input_output_aliases={6: 0} if slot else {},
        compiler_params=pltpu.CompilerParams(vmem_limit_bytes=32 * 1024 * 1024),
        cost_estimate=pl.CostEstimate(
            flops=2 * tok_rows * features * rows,
            bytes_accessed=4 * tok_rows * features,
            transcendentals=rows * tok_rows * KV_HEADS * GROUP // 2,
        ),
    )(span_ids, queries, piece, *state, *([out] if slot else []))


def fold(count, shifts, pieces, state, end, span_ids, queries):
    vmem = pl.BlockSpec(memory_space=pltpu.VMEM)
    tok_rows, features = queries.shape
    slot_rows = GROUP * (tok_rows // 2)
    begin = state is None
    state = [] if begin else list(state)
    if end:
        out_shape = jax.ShapeDtypeStruct((tok_rows, features), jnp.bfloat16)
    else:
        row = jax.ShapeDtypeStruct((2, KV_HEADS, 1, slot_rows), jnp.float32)
        out_shape = [row, row, jax.ShapeDtypeStruct((2, KV_HEADS, HEAD_DIM, slot_rows), jnp.float32)]
    keys = (len(pieces) // 2) * tok_rows
    return pl.pallas_call(
        functools.partial(attend, count, tuple(shifts), begin, end),
        out_shape=out_shape,
        in_specs=[vmem] * (2 + len(pieces) + len(state)),
        out_specs=vmem if end else [vmem] * 3,
        compiler_params=pltpu.CompilerParams(vmem_limit_bytes=32 * 1024 * 1024),
        cost_estimate=pl.CostEstimate(
            flops=2 * keys * features * tok_rows,
            bytes_accessed=2 * keys * 2 * WIDTH + 4 * tok_rows * features,
            transcendentals=keys * tok_rows * KV_HEADS * GROUP // 2,
        ),
    )(span_ids, queries, *pieces, *state)


def per_device(queries, keyvals, span_ids):
    count = lax.axis_size("ctx")
    rows = queries.shape[1] // 2
    order = ring_order(count)
    ahead = [(order[i], order[(i + 1) % count]) for i in range(count)]
    back = [(b, a) for a, b in ahead]

    flat = lax.optimization_barrier(keyvals[0].reshape(2 * rows, 2 * WIDTH))
    own = [flat[:rows], flat[rows:]]
    up, down = own, own
    last = count // 2
    held, state = ([], own), None
    for step in range(1, last + 1):
        if step > 1:
            state = fold(count, *held, state, False, span_ids, queries[0])
            if step == 2:
                up[0], *state = lax.optimization_barrier((up[0], *state))
            held = shifts, pieces
        if 2 * step < count:
            up = [lax.ppermute(piece, "ctx", ahead) for piece in up]
            down = [lax.ppermute(piece, "ctx", back) for piece in down]
            shifts, pieces = [-step, step], up + down
        else:
            shifts = [-step]
            pieces = [lax.ppermute(up[0], "ctx", ahead), lax.ppermute(down[1], "ctx", back)]
    if last:
        state = fold(count, *held, state, False, span_ids, queries[0])
        held = shifts, pieces
    if count % 2:
        return fold(count, *held, state, True, span_ids, queries[0])[None]
    out, *state = end(count, shifts[0], 0, pieces[0], state, None, span_ids, queries[0])
    return end(count, shifts[0], 1, pieces[1], state, out, span_ids, queries[0])[None]


def solution(mesh):
    in_specs = (P("fsdp", "ctx", None), P("fsdp", "ctx", None, None), P("fsdp", None))
    out_specs = P("fsdp", "ctx", None)
    return jax.shard_map(
        per_device, mesh=mesh, in_specs=in_specs, out_specs=out_specs, check_vma=False
    )
```

```python
import functools
import math

import jax
import jax.numpy as jnp
from jax import lax
from jax.experimental import pallas as pl
from jax.experimental.pallas import tpu as pltpu
from jax.sharding import PartitionSpec as P

KV_HEADS = 4
GROUP = 4
HEAD_DIM = 128
WIDTH = KV_HEADS * HEAD_DIM
NT = (((1,), (1,)), ((), ()))
TN = (((0,), (0,)), ((), ()))


def ring_order(count):
    return [i for i in range(count) if i % 2 == 0] + [i for i in reversed(range(count)) if i % 2]


def ring_member(place, count):
    half = (count + 1) // 2
    return jnp.where(place < half, 2 * place, 2 * (count - 1 - place) + 1)


def ring_place(member, count):
    return jnp.where(member % 2 == 0, member // 2, count - 1 - member // 2)


def key(piece, j):
    return piece[:, j * HEAD_DIM : (j + 1) * HEAD_DIM]


def value(piece, j):
    return piece[:, WIDTH + j * HEAD_DIM : WIDTH + (j + 1) * HEAD_DIM]


def read_queries(q_ref, slot, rows, j):
    start = slot * rows if isinstance(slot, int) else pl.multiple_of(slot * rows, rows)
    return jnp.concatenate(
        [
            q_ref[pl.ds(start, rows), (j * GROUP + g) * HEAD_DIM : (j * GROUP + g + 1) * HEAD_DIM]
            for g in range(GROUP)
        ],
        axis=0,
    )


def scores(k, q):
    scale = math.log2(math.e) / math.sqrt(HEAD_DIM)
    return lax.dot_general(k, q, NT, preferred_element_type=jnp.float32) * scale


def weigh(v, p):
    return lax.dot_general(v, p, TN, preferred_element_type=jnp.float32)


def comes_before(count, shifts, span_ref):
    place = ring_place(lax.axis_index("ctx"), count)
    table = span_ref[...].astype(jnp.float32)
    lane = lax.broadcasted_iota(jnp.int32, table.shape, 1)

    def span_of(shift):
        member = ring_member((place + shift + count) % count, count)
        return jnp.sum(jnp.where(lane == 2 * member, table, 0.0))

    own_span = span_of(0)
    return [span_of(shift) < own_span for shift in shifts]


def normalized(total, acc):
    return (acc * (1.0 / total)).astype(jnp.bfloat16).T


def attend(count, shifts, begin, end, span_ref, q_ref, *refs):
    refs = list(refs)
    chunks = [(refs.pop(0), refs.pop(0)) for _ in range(len(shifts) + begin)]
    if not begin:
        top_in, total_in, acc_in = refs.pop(0), refs.pop(0), refs.pop(0)
    if end:
        out_ref = refs.pop(0)
    else:
        top_out, total_out, acc_out = refs
    rows = chunks[0][0].shape[0]
    slot_rows = GROUP * rows

    def queries(slot, j):
        return read_queries(q_ref, slot, rows, j)

    heads = range(KV_HEADS)
    result = {}
    if begin:
        early, late = chunks.pop(0)
        key_row = lax.broadcasted_iota(jnp.int32, (rows, slot_rows), 0)
        query_row = lax.broadcasted_iota(jnp.int32, (rows, slot_rows), 1) % rows
        causal = key_row <= query_row
        for j in heads:
            q = queries(0, j)
            s = jnp.where(causal, scores(key(early, j), q), -1e30)
            new = jnp.max(s, axis=0, keepdims=True)
            p = jnp.exp2(s - new)
            result[0, j] = new, jnp.sum(p, axis=0, keepdims=True), weigh(value(early, j), p.astype(jnp.bfloat16))
            q = queries(1, j)
            k = jnp.concatenate([key(early, j), key(late, j)], axis=0)
            v = jnp.concatenate([value(early, j), value(late, j)], axis=0)
            s = scores(k, q)
            s = jnp.concatenate([s[:rows], jnp.where(causal, s[rows:], -1e30)], axis=0)
            new = jnp.max(s, axis=0, keepdims=True)
            p = jnp.exp2(s - new)
            result[1, j] = new, jnp.sum(p, axis=0, keepdims=True), weigh(v, p.astype(jnp.bfloat16))
    else:
        n = len(shifts)
        befores = comes_before(count, shifts, span_ref)
        slots = [jnp.where(before, 0, 1) for before in befores]
        picked = [
            jnp.where(before, early[...], late[...]) for before, (early, late) in zip(befores, chunks)
        ]
        full, part = {}, {}
        for j in heads:
            k = jnp.concatenate([key(early, j) for early, _ in chunks], axis=0)
            full[j] = scores(k, queries(1, j))
            part[j] = [scores(key(picked[i], j), queries(slots[i], j)) for i in range(n)]
        for j in heads:
            old = [top_in[0, j], top_in[1, j]]
            most = [jnp.max(s, axis=0, keepdims=True) for s in part[j]]
            new = [old[0], jnp.maximum(old[1], jnp.max(full[j], axis=0, keepdims=True))]
            for i in range(n):
                new[0] = jnp.maximum(new[0], jnp.where(befores[i], most[i], -1e30))
                new[1] = jnp.maximum(new[1], jnp.where(befores[i], -1e30, most[i]))
            p = jnp.exp2(full[j] - new[1])
            shrink = [jnp.exp2(old[slot] - new[slot]) for slot in range(2)]
            added = [total_in[0, j] * shrink[0], total_in[1, j] * shrink[1] + jnp.sum(p, axis=0, keepdims=True)]
            weights = [[], [p.astype(jnp.bfloat16)]]
            values = [[value(picked[i], j) for i in range(n)], [value(early, j) for early, _ in chunks]]
            values[1] += values[0]
            for i in range(n):
                p = jnp.exp2(part[j][i] - jnp.where(befores[i], new[0], new[1]))
                t = jnp.sum(p, axis=0, keepdims=True)
                p = p.astype(jnp.bfloat16)
                zero = jnp.zeros_like(p)
                added[0] = added[0] + jnp.where(befores[i], t, 0.0)
                added[1] = added[1] + jnp.where(befores[i], 0.0, t)
                weights[0].append(jnp.where(befores[i], p, zero))
                weights[1].append(jnp.where(befores[i], zero, p))
            for slot in range(2):
                update = weigh(
                    jnp.concatenate(values[slot], axis=0), jnp.concatenate(weights[slot], axis=0)
                )
                result[slot, j] = new[slot], added[slot], acc_in[slot, j] * shrink[slot] + update

    for (slot, j), (new, added, update) in result.items():
        if end:
            done = normalized(added, update)
            for g in range(GROUP):
                h = j * GROUP + g
                out_ref[
                    slot * rows : (slot + 1) * rows, h * HEAD_DIM : (h + 1) * HEAD_DIM
                ] = done[g * rows : (g + 1) * rows]
        else:
            top_out[slot, j] = new
            total_out[slot, j] = added
            acc_out[slot, j] = update


def fold_heads(old, piece, queries, counts):
    heads = range(KV_HEADS)
    s = [scores(key(piece, j), queries[j]) for j in heads]
    most = [jnp.max(s[j], axis=0, keepdims=True) for j in heads]
    if counts is not None:
        most = [jnp.where(counts, most[j], -1e30) for j in heads]
    new = [jnp.maximum(old[j][0], most[j]) for j in heads]
    if counts is not None:
        s = [jnp.where(counts, s[j], -1e30) for j in heads]
    p = [jnp.exp2(s[j] - new[j]) for j in heads]
    update = [weigh(value(piece, j), p[j].astype(jnp.bfloat16)) for j in heads]
    shrink = [jnp.exp2(old[j][0] - new[j]) for j in heads]
    total = [old[j][1] * shrink[j] + jnp.sum(p[j], axis=0, keepdims=True) for j in heads]
    acc = [old[j][2] * shrink[j] + update[j] for j in heads]
    return list(zip(new, total, acc))


def finish(count, shift, slot, span_ref, q_ref, piece, *refs):
    refs = list(refs)
    top_in, total_in, acc_in = refs.pop(0), refs.pop(0), refs.pop(0)
    rows = piece.shape[0]
    if slot:
        refs.pop(0)
        out_ref, done, sems = refs
        before = span_ref[0:1, 0:1][0, 0] > 0.0
    else:
        out_ref, top_out, total_out, acc_out, flag, done, sems = refs
        (before,) = comes_before(count, [shift], span_ref)
        flag[...] = jnp.where(before, jnp.ones(flag.shape, jnp.float32), 0.0)

    def folded(i, counts):
        old = [(top_in[i, j], total_in[i, j], acc_in[i, j]) for j in range(KV_HEADS)]
        queries = [read_queries(q_ref, i, rows, j) for j in range(KV_HEADS)]
        return fold_heads(old, piece, queries, counts)

    def write(i, states):
        copies = []
        for j in range(KV_HEADS):
            _, total, acc = states[j]
            result = normalized(total, acc)
            for g in range(GROUP):
                h = j * GROUP + g
                done[i, :, h * HEAD_DIM : (h + 1) * HEAD_DIM] = result[g * rows : (g + 1) * rows]
            columns = slice(j * GROUP * HEAD_DIM, (j + 1) * GROUP * HEAD_DIM)
            copies.append(
                pltpu.make_async_copy(
                    done.at[i, :, columns], out_ref.at[i * rows : (i + 1) * rows, columns], sems.at[i, j]
                )
            )
            copies[-1].start()
        return copies

    if slot:

        @pl.when(jnp.logical_not(before))
        def _():
            for copy in write(1, folded(1, None)):
                copy.wait()

        return

    copies = write(0, folded(0, before))
    states = folded(1, None)
    for j in range(KV_HEADS):
        top_out[1, j], total_out[1, j], acc_out[1, j] = states[j]

    @pl.when(before)
    def _():
        kept = [(top_out[1, j], total_out[1, j], acc_out[1, j]) for j in range(KV_HEADS)]
        for copy in write(1, kept):
            copy.wait()

    for copy in copies:
        copy.wait()


def end(count, shift, slot, piece, state, out, span_ids, queries):
    tok_rows, features = queries.shape
    rows = tok_rows // 2
    vmem, hbm = pl.BlockSpec(memory_space=pltpu.VMEM), pl.BlockSpec(memory_space=pltpu.HBM)
    result = jax.ShapeDtypeStruct((tok_rows, features), queries.dtype)
    like = [jax.ShapeDtypeStruct(part.shape, part.dtype) for part in state]
    return pl.pallas_call(
        functools.partial(finish, count, shift, slot),
        out_shape=result if slot else [result, *like, jax.ShapeDtypeStruct((8, 128), jnp.float32)],
        in_specs=[vmem] * 6 + [hbm] * slot,
        out_specs=hbm if slot else [hbm] + [vmem] * 4,
        scratch_shapes=[
            pltpu.VMEM((2, rows, features), queries.dtype),
            pltpu.SemaphoreType.DMA((2, KV_HEADS)),
        ],
        input_output_aliases={6: 0} if slot else {},
        compiler_params=pltpu.CompilerParams(vmem_limit_bytes=32 * 1024 * 1024),
        cost_estimate=pl.CostEstimate(
            flops=2 * tok_rows * features * rows,
            bytes_accessed=4 * tok_rows * features,
            transcendentals=rows * tok_rows * KV_HEADS * GROUP // 2,
        ),
    )(span_ids, queries, piece, *state, *([out] if slot else []))


def fold(count, shifts, pieces, state, end, span_ids, queries):
    vmem = pl.BlockSpec(memory_space=pltpu.VMEM)
    tok_rows, features = queries.shape
    slot_rows = GROUP * (tok_rows // 2)
    begin = state is None
    state = [] if begin else list(state)
    if end:
        out_shape = jax.ShapeDtypeStruct((tok_rows, features), jnp.bfloat16)
    else:
        row = jax.ShapeDtypeStruct((2, KV_HEADS, 1, slot_rows), jnp.float32)
        out_shape = [row, row, jax.ShapeDtypeStruct((2, KV_HEADS, HEAD_DIM, slot_rows), jnp.float32)]
    keys = (len(pieces) // 2) * tok_rows
    return pl.pallas_call(
        functools.partial(attend, count, tuple(shifts), begin, end),
        out_shape=out_shape,
        in_specs=[vmem] * (2 + len(pieces) + len(state)),
        out_specs=vmem if end else [vmem] * 3,
        compiler_params=pltpu.CompilerParams(vmem_limit_bytes=32 * 1024 * 1024),
        cost_estimate=pl.CostEstimate(
            flops=2 * keys * features * tok_rows,
            bytes_accessed=2 * keys * 2 * WIDTH + 4 * tok_rows * features,
            transcendentals=keys * tok_rows * KV_HEADS * GROUP // 2,
        ),
    )(span_ids, queries, *pieces, *state)


def per_device(queries, keyvals, span_ids):
    count = lax.axis_size("ctx")
    rows = queries.shape[1] // 2
    order = ring_order(count)
    ahead = [(order[i], order[(i + 1) % count]) for i in range(count)]
    back = [(b, a) for a, b in ahead]

    flat = lax.optimization_barrier(keyvals[0].reshape(2 * rows, 2 * WIDTH))
    own = [flat[:rows], flat[rows:]]
    up, down = own, own
    last = count // 2
    held, state = ([], own), None
    for step in range(1, last + 1):
        if step > 1:
            state = fold(count, *held, state, False, span_ids, queries[0])
            if step == 2:
                up[0], *state = lax.optimization_barrier((up[0], *state))
            held = shifts, pieces
        if 2 * step < count:
            up = [lax.ppermute(piece, "ctx", ahead) for piece in up]
            down = [lax.ppermute(piece, "ctx", back) for piece in down]
            shifts, pieces = [-step, step], up + down
        else:
            shifts = [-step]
            pieces = [lax.ppermute(up[0], "ctx", ahead), lax.ppermute(down[1], "ctx", back)]
    if last:
        state = fold(count, *held, state, False, span_ids, queries[0])
        held = shifts, pieces
    if count % 2:
        return fold(count, *held, state, True, span_ids, queries[0])[None]
    out, *state, encloses = end(count, shifts[0], 0, pieces[0], state, None, span_ids, queries[0])
    return end(count, shifts[0], 1, pieces[1], state, out, encloses, queries[0])[None]


def solution(mesh):
    in_specs = (P("fsdp", "ctx", None), P("fsdp", "ctx", None, None), P("fsdp", None))
    out_specs = P("fsdp", "ctx", None)
    return jax.shard_map(
        per_device, mesh=mesh, in_specs=in_specs, out_specs=out_specs, check_vma=False
    )
```

```python
import functools
import math

import jax
import jax.numpy as jnp
from jax import lax
from jax.experimental import pallas as pl
from jax.experimental.pallas import tpu as pltpu
from jax.sharding import PartitionSpec as P

KV_HEADS = 4
GROUP = 4
HEAD_DIM = 128
WIDTH = KV_HEADS * HEAD_DIM
NT = (((1,), (1,)), ((), ()))
TN = (((0,), (0,)), ((), ()))


def ring_order(count):
    return [i for i in range(count) if i % 2 == 0] + [i for i in reversed(range(count)) if i % 2]


def ring_member(place, count):
    half = (count + 1) // 2
    return jnp.where(place < half, 2 * place, 2 * (count - 1 - place) + 1)


def ring_place(member, count):
    return jnp.where(member % 2 == 0, member // 2, count - 1 - member // 2)


def key(piece, j):
    return piece[:, j * HEAD_DIM : (j + 1) * HEAD_DIM]


def value(piece, j):
    return piece[:, WIDTH + j * HEAD_DIM : WIDTH + (j + 1) * HEAD_DIM]


def read_queries(q_ref, slot, rows, j):
    start = slot * rows if isinstance(slot, int) else pl.multiple_of(slot * rows, rows)
    return jnp.concatenate(
        [
            q_ref[pl.ds(start, rows), (j * GROUP + g) * HEAD_DIM : (j * GROUP + g + 1) * HEAD_DIM]
            for g in range(GROUP)
        ],
        axis=0,
    )


def scores(k, q):
    scale = math.log2(math.e) / math.sqrt(HEAD_DIM)
    return lax.dot_general(k, q, NT, preferred_element_type=jnp.float32) * scale


def weigh(v, p):
    return lax.dot_general(v, p, TN, preferred_element_type=jnp.float32)


def comes_before(count, shifts, span_ref):
    place = ring_place(lax.axis_index("ctx"), count)
    table = span_ref[...].astype(jnp.float32)
    lane = lax.broadcasted_iota(jnp.int32, table.shape, 1)

    def span_of(shift):
        member = ring_member((place + shift + count) % count, count)
        return jnp.sum(jnp.where(lane == 2 * member, table, 0.0))

    own_span = span_of(0)
    return [span_of(shift) < own_span for shift in shifts]


def normalized(total, acc):
    return (acc * (1.0 / total)).astype(jnp.bfloat16).T


def attend(count, shifts, begin, end, span_ref, q_ref, *refs):
    refs = list(refs)
    chunks = [(refs.pop(0), refs.pop(0)) for _ in range(len(shifts) + begin)]
    if not begin:
        top_in, total_in, acc_in = refs.pop(0), refs.pop(0), refs.pop(0)
    if end:
        out_ref = refs.pop(0)
    else:
        top_out, total_out, acc_out = refs
    rows = chunks[0][0].shape[0]
    slot_rows = GROUP * rows

    def queries(slot, j):
        return read_queries(q_ref, slot, rows, j)

    heads = range(KV_HEADS)
    result = {}
    if begin:
        early, late = chunks.pop(0)
        key_row = lax.broadcasted_iota(jnp.int32, (rows, slot_rows), 0)
        query_row = lax.broadcasted_iota(jnp.int32, (rows, slot_rows), 1) % rows
        causal = key_row <= query_row
        for j in heads:
            q = queries(0, j)
            s = jnp.where(causal, scores(key(early, j), q), -1e30)
            new = jnp.max(s, axis=0, keepdims=True)
            p = jnp.exp2(s - new)
            result[0, j] = new, jnp.sum(p, axis=0, keepdims=True), weigh(value(early, j), p.astype(jnp.bfloat16))
            q = queries(1, j)
            k = jnp.concatenate([key(early, j), key(late, j)], axis=0)
            v = jnp.concatenate([value(early, j), value(late, j)], axis=0)
            s = scores(k, q)
            s = jnp.concatenate([s[:rows], jnp.where(causal, s[rows:], -1e30)], axis=0)
            new = jnp.max(s, axis=0, keepdims=True)
            p = jnp.exp2(s - new)
            result[1, j] = new, jnp.sum(p, axis=0, keepdims=True), weigh(v, p.astype(jnp.bfloat16))
    else:
        n = len(shifts)
        befores = comes_before(count, shifts, span_ref)
        slots = [jnp.where(before, 0, 1) for before in befores]
        picked = [
            jnp.where(before, early[...], late[...]) for before, (early, late) in zip(befores, chunks)
        ]
        full, part = {}, {}
        for j in heads:
            k = jnp.concatenate([key(early, j) for early, _ in chunks], axis=0)
            full[j] = scores(k, queries(1, j))
            part[j] = [scores(key(picked[i], j), queries(slots[i], j)) for i in range(n)]
        for j in heads:
            old = [top_in[0, j], top_in[1, j]]
            most = [jnp.max(s, axis=0, keepdims=True) for s in part[j]]
            new = [old[0], jnp.maximum(old[1], jnp.max(full[j], axis=0, keepdims=True))]
            for i in range(n):
                new[0] = jnp.maximum(new[0], jnp.where(befores[i], most[i], -1e30))
                new[1] = jnp.maximum(new[1], jnp.where(befores[i], -1e30, most[i]))
            p = jnp.exp2(full[j] - new[1])
            shrink = [jnp.exp2(old[slot] - new[slot]) for slot in range(2)]
            added = [total_in[0, j] * shrink[0], total_in[1, j] * shrink[1] + jnp.sum(p, axis=0, keepdims=True)]
            weights = [[], [p.astype(jnp.bfloat16)]]
            values = [[value(picked[i], j) for i in range(n)], [value(early, j) for early, _ in chunks]]
            values[1] += values[0]
            for i in range(n):
                p = jnp.exp2(part[j][i] - jnp.where(befores[i], new[0], new[1]))
                t = jnp.sum(p, axis=0, keepdims=True)
                p = p.astype(jnp.bfloat16)
                zero = jnp.zeros_like(p)
                added[0] = added[0] + jnp.where(befores[i], t, 0.0)
                added[1] = added[1] + jnp.where(befores[i], 0.0, t)
                weights[0].append(jnp.where(befores[i], p, zero))
                weights[1].append(jnp.where(befores[i], zero, p))
            for slot in range(2):
                update = weigh(
                    jnp.concatenate(values[slot], axis=0), jnp.concatenate(weights[slot], axis=0)
                )
                result[slot, j] = new[slot], added[slot], acc_in[slot, j] * shrink[slot] + update

    for (slot, j), (new, added, update) in result.items():
        if end:
            done = normalized(added, update)
            for g in range(GROUP):
                h = j * GROUP + g
                out_ref[
                    slot * rows : (slot + 1) * rows, h * HEAD_DIM : (h + 1) * HEAD_DIM
                ] = done[g * rows : (g + 1) * rows]
        else:
            top_out[slot, j] = new
            total_out[slot, j] = added
            acc_out[slot, j] = update


def fold_heads(old, piece, queries, counts):
    heads = range(KV_HEADS)
    s = [scores(key(piece, j), queries[j]) for j in heads]
    most = [jnp.max(s[j], axis=0, keepdims=True) for j in heads]
    if counts is not None:
        most = [jnp.where(counts, most[j], -1e30) for j in heads]
    new = [jnp.maximum(old[j][0], most[j]) for j in heads]
    if counts is not None:
        s = [jnp.where(counts, s[j], -1e30) for j in heads]
    p = [jnp.exp2(s[j] - new[j]) for j in heads]
    update = [weigh(value(piece, j), p[j].astype(jnp.bfloat16)) for j in heads]
    shrink = [jnp.exp2(old[j][0] - new[j]) for j in heads]
    total = [old[j][1] * shrink[j] + jnp.sum(p[j], axis=0, keepdims=True) for j in heads]
    acc = [old[j][2] * shrink[j] + update[j] for j in heads]
    return list(zip(new, total, acc))


def finish(count, shift, slot, span_ref, q_ref, piece, *refs):
    refs = list(refs)
    top_in, total_in, acc_in = refs.pop(0), refs.pop(0), refs.pop(0)
    rows = piece.shape[0]
    if slot:
        refs.pop(0)
        out_ref, done, sems = refs
        before = span_ref[0:1, 0:1][0, 0] > 0.0
    else:
        out_ref, top_out, total_out, acc_out, flag, done, sems = refs
        (before,) = comes_before(count, [shift], span_ref)
        flag[...] = jnp.where(before, jnp.ones(flag.shape, jnp.float32), 0.0)

    def folded(i, counts):
        old = [(top_in[i, j], total_in[i, j], acc_in[i, j]) for j in range(KV_HEADS)]
        queries = [read_queries(q_ref, i, rows, j) for j in range(KV_HEADS)]
        return fold_heads(old, piece, queries, counts)

    def write(i, states):
        copies = []
        for j in range(KV_HEADS):
            _, total, acc = states[j]
            result = normalized(total, acc)
            for g in range(GROUP):
                h = j * GROUP + g
                done[i, :, h * HEAD_DIM : (h + 1) * HEAD_DIM] = result[g * rows : (g + 1) * rows]
            columns = slice(j * GROUP * HEAD_DIM, (j + 1) * GROUP * HEAD_DIM)
            copies.append(
                pltpu.make_async_copy(
                    done.at[i, :, columns], out_ref.at[i * rows : (i + 1) * rows, columns], sems.at[i, j]
                )
            )
            copies[-1].start()
        return copies

    if slot:

        @pl.when(jnp.logical_not(before))
        def _():
            for copy in write(1, folded(1, None)):
                copy.wait()

        return

    @pl.when(before)
    def _():
        copies = write(0, folded(0, None)) + write(1, folded(1, None))
        for copy in copies:
            copy.wait()

    @pl.when(jnp.logical_not(before))
    def _():
        copies = write(0, [(top_in[0, j], total_in[0, j], acc_in[0, j]) for j in range(KV_HEADS)])
        states = folded(1, None)
        for j in range(KV_HEADS):
            top_out[1, j], total_out[1, j], acc_out[1, j] = states[j]
        for copy in copies:
            copy.wait()


def end(count, shift, slot, piece, state, out, span_ids, queries):
    tok_rows, features = queries.shape
    rows = tok_rows // 2
    vmem, hbm = pl.BlockSpec(memory_space=pltpu.VMEM), pl.BlockSpec(memory_space=pltpu.HBM)
    result = jax.ShapeDtypeStruct((tok_rows, features), queries.dtype)
    like = [jax.ShapeDtypeStruct(part.shape, part.dtype) for part in state]
    return pl.pallas_call(
        functools.partial(finish, count, shift, slot),
        out_shape=result if slot else [result, *like, jax.ShapeDtypeStruct((8, 128), jnp.float32)],
        in_specs=[vmem] * 6 + [hbm] * slot,
        out_specs=hbm if slot else [hbm] + [vmem] * 4,
        scratch_shapes=[
            pltpu.VMEM((2, rows, features), queries.dtype),
            pltpu.SemaphoreType.DMA((2, KV_HEADS)),
        ],
        input_output_aliases={6: 0} if slot else {},
        compiler_params=pltpu.CompilerParams(vmem_limit_bytes=32 * 1024 * 1024),
        cost_estimate=pl.CostEstimate(
            flops=2 * tok_rows * features * rows,
            bytes_accessed=4 * tok_rows * features,
            transcendentals=rows * tok_rows * KV_HEADS * GROUP // 2,
        ),
    )(span_ids, queries, piece, *state, *([out] if slot else []))


def fold(count, shifts, pieces, state, end, span_ids, queries):
    vmem = pl.BlockSpec(memory_space=pltpu.VMEM)
    tok_rows, features = queries.shape
    slot_rows = GROUP * (tok_rows // 2)
    begin = state is None
    state = [] if begin else list(state)
    if end:
        out_shape = jax.ShapeDtypeStruct((tok_rows, features), jnp.bfloat16)
    else:
        row = jax.ShapeDtypeStruct((2, KV_HEADS, 1, slot_rows), jnp.float32)
        out_shape = [row, row, jax.ShapeDtypeStruct((2, KV_HEADS, HEAD_DIM, slot_rows), jnp.float32)]
    keys = (len(pieces) // 2) * tok_rows
    return pl.pallas_call(
        functools.partial(attend, count, tuple(shifts), begin, end),
        out_shape=out_shape,
        in_specs=[vmem] * (2 + len(pieces) + len(state)),
        out_specs=vmem if end else [vmem] * 3,
        compiler_params=pltpu.CompilerParams(vmem_limit_bytes=32 * 1024 * 1024),
        cost_estimate=pl.CostEstimate(
            flops=2 * keys * features * tok_rows,
            bytes_accessed=2 * keys * 2 * WIDTH + 4 * tok_rows * features,
            transcendentals=keys * tok_rows * KV_HEADS * GROUP // 2,
        ),
    )(span_ids, queries, *pieces, *state)


def per_device(queries, keyvals, span_ids):
    count = lax.axis_size("ctx")
    rows = queries.shape[1] // 2
    order = ring_order(count)
    ahead = [(order[i], order[(i + 1) % count]) for i in range(count)]
    back = [(b, a) for a, b in ahead]

    flat = lax.optimization_barrier(keyvals[0].reshape(2 * rows, 2 * WIDTH))
    own = [flat[:rows], flat[rows:]]
    up, down = own, own
    last = count // 2
    held, state = ([], own), None
    for step in range(1, last + 1):
        if step > 1:
            state = fold(count, *held, state, False, span_ids, queries[0])
            if step == 2:
                up[0], *state = lax.optimization_barrier((up[0], *state))
            held = shifts, pieces
        if 2 * step < count:
            up = [lax.ppermute(piece, "ctx", ahead) for piece in up]
            down = [lax.ppermute(piece, "ctx", back) for piece in down]
            shifts, pieces = [-step, step], up + down
        else:
            shifts = [-step]
            pieces = [lax.ppermute(up[0], "ctx", ahead), lax.ppermute(down[1], "ctx", back)]
    if last:
        state = fold(count, *held, state, False, span_ids, queries[0])
        held = shifts, pieces
    if count % 2:
        return fold(count, *held, state, True, span_ids, queries[0])[None]
    out, *state, encloses = end(count, shifts[0], 0, pieces[0], state, None, span_ids, queries[0])
    return end(count, shifts[0], 1, pieces[1], state, out, encloses, queries[0])[None]


def solution(mesh):
    in_specs = (P("fsdp", "ctx", None), P("fsdp", "ctx", None, None), P("fsdp", None))
    out_specs = P("fsdp", "ctx", None)
    return jax.shard_map(
        per_device, mesh=mesh, in_specs=in_specs, out_specs=out_specs, check_vma=False
    )
```

```python
import functools
import math

import jax
import jax.numpy as jnp
from jax import lax
from jax.experimental import pallas as pl
from jax.experimental.pallas import tpu as pltpu
from jax.sharding import PartitionSpec as P

KV_HEADS = 4
GROUP = 4
HEAD_DIM = 128
WIDTH = KV_HEADS * HEAD_DIM
NT = (((1,), (1,)), ((), ()))
TN = (((0,), (0,)), ((), ()))


def ring_order(count):
    return [i for i in range(count) if i % 2 == 0] + [i for i in reversed(range(count)) if i % 2]


def ring_member(place, count):
    half = (count + 1) // 2
    return jnp.where(place < half, 2 * place, 2 * (count - 1 - place) + 1)


def ring_place(member, count):
    return jnp.where(member % 2 == 0, member // 2, count - 1 - member // 2)


def key(piece, j):
    return piece[:, j * HEAD_DIM : (j + 1) * HEAD_DIM]


def value(piece, j):
    return piece[:, WIDTH + j * HEAD_DIM : WIDTH + (j + 1) * HEAD_DIM]


def read_queries(q_ref, slot, rows, j):
    start = slot * rows if isinstance(slot, int) else pl.multiple_of(slot * rows, rows)
    return jnp.concatenate(
        [
            q_ref[pl.ds(start, rows), (j * GROUP + g) * HEAD_DIM : (j * GROUP + g + 1) * HEAD_DIM]
            for g in range(GROUP)
        ],
        axis=0,
    )


def scores(k, q):
    scale = math.log2(math.e) / math.sqrt(HEAD_DIM)
    return lax.dot_general(k, q, NT, preferred_element_type=jnp.float32) * scale


def weigh(v, p):
    return lax.dot_general(v, p, TN, preferred_element_type=jnp.float32)


def comes_before(count, shifts, span_ref):
    place = ring_place(lax.axis_index("ctx"), count)
    table = span_ref[...].astype(jnp.float32)
    lane = lax.broadcasted_iota(jnp.int32, table.shape, 1)

    def span_of(shift):
        member = ring_member((place + shift + count) % count, count)
        return jnp.sum(jnp.where(lane == 2 * member, table, 0.0))

    own_span = span_of(0)
    return [span_of(shift) < own_span for shift in shifts]


def normalized(total, acc):
    return (acc * (1.0 / total)).astype(jnp.bfloat16).T


def attend(count, shifts, begin, end, span_ref, q_ref, *refs):
    refs = list(refs)
    chunks = [(refs.pop(0), refs.pop(0)) for _ in range(len(shifts) + begin)]
    if not begin:
        top_in, total_in, acc_in = refs.pop(0), refs.pop(0), refs.pop(0)
    if end:
        out_ref = refs.pop(0)
    else:
        top_out, total_out, acc_out = refs
    rows = chunks[0][0].shape[0]
    slot_rows = GROUP * rows

    def queries(slot, j):
        return read_queries(q_ref, slot, rows, j)

    heads = range(KV_HEADS)
    result = {}
    if begin:
        early, late = chunks.pop(0)
        key_row = lax.broadcasted_iota(jnp.int32, (rows, slot_rows), 0)
        query_row = lax.broadcasted_iota(jnp.int32, (rows, slot_rows), 1) % rows
        causal = key_row <= query_row
        for j in heads:
            q = queries(0, j)
            s = jnp.where(causal, scores(key(early, j), q), -1e30)
            new = jnp.max(s, axis=0, keepdims=True)
            p = jnp.exp2(s - new)
            result[0, j] = new, jnp.sum(p, axis=0, keepdims=True), weigh(value(early, j), p.astype(jnp.bfloat16))
            q = queries(1, j)
            k = jnp.concatenate([key(early, j), key(late, j)], axis=0)
            v = jnp.concatenate([value(early, j), value(late, j)], axis=0)
            s = scores(k, q)
            s = jnp.concatenate([s[:rows], jnp.where(causal, s[rows:], -1e30)], axis=0)
            new = jnp.max(s, axis=0, keepdims=True)
            p = jnp.exp2(s - new)
            result[1, j] = new, jnp.sum(p, axis=0, keepdims=True), weigh(v, p.astype(jnp.bfloat16))
    else:
        n = len(shifts)
        befores = comes_before(count, shifts, span_ref)
        slots = [jnp.where(before, 0, 1) for before in befores]
        picked = [
            jnp.where(before, early[...], late[...]) for before, (early, late) in zip(befores, chunks)
        ]
        full, part = {}, {}
        for j in heads:
            k = jnp.concatenate([key(early, j) for early, _ in chunks], axis=0)
            full[j] = scores(k, queries(1, j))
            part[j] = [scores(key(picked[i], j), queries(slots[i], j)) for i in range(n)]
        for j in heads:
            old = [top_in[0, j], top_in[1, j]]
            most = [jnp.max(s, axis=0, keepdims=True) for s in part[j]]
            new = [old[0], jnp.maximum(old[1], jnp.max(full[j], axis=0, keepdims=True))]
            for i in range(n):
                new[0] = jnp.maximum(new[0], jnp.where(befores[i], most[i], -1e30))
                new[1] = jnp.maximum(new[1], jnp.where(befores[i], -1e30, most[i]))
            p = jnp.exp2(full[j] - new[1])
            shrink = [jnp.exp2(old[slot] - new[slot]) for slot in range(2)]
            added = [total_in[0, j] * shrink[0], total_in[1, j] * shrink[1] + jnp.sum(p, axis=0, keepdims=True)]
            weights = [[], [p.astype(jnp.bfloat16)]]
            values = [[value(picked[i], j) for i in range(n)], [value(early, j) for early, _ in chunks]]
            values[1] += values[0]
            for i in range(n):
                p = jnp.exp2(part[j][i] - jnp.where(befores[i], new[0], new[1]))
                t = jnp.sum(p, axis=0, keepdims=True)
                p = p.astype(jnp.bfloat16)
                zero = jnp.zeros_like(p)
                added[0] = added[0] + jnp.where(befores[i], t, 0.0)
                added[1] = added[1] + jnp.where(befores[i], 0.0, t)
                weights[0].append(jnp.where(befores[i], p, zero))
                weights[1].append(jnp.where(befores[i], zero, p))
            for slot in range(2):
                update = weigh(
                    jnp.concatenate(values[slot], axis=0), jnp.concatenate(weights[slot], axis=0)
                )
                result[slot, j] = new[slot], added[slot], acc_in[slot, j] * shrink[slot] + update

    for (slot, j), (new, added, update) in result.items():
        if end:
            done = normalized(added, update)
            for g in range(GROUP):
                h = j * GROUP + g
                out_ref[
                    slot * rows : (slot + 1) * rows, h * HEAD_DIM : (h + 1) * HEAD_DIM
                ] = done[g * rows : (g + 1) * rows]
        else:
            top_out[slot, j] = new
            total_out[slot, j] = added
            acc_out[slot, j] = update


def fold_heads(old, piece, queries, counts):
    heads = range(KV_HEADS)
    s = [scores(key(piece, j), queries[j]) for j in heads]
    most = [jnp.max(s[j], axis=0, keepdims=True) for j in heads]
    if counts is not None:
        most = [jnp.where(counts, most[j], -1e30) for j in heads]
    new = [jnp.maximum(old[j][0], most[j]) for j in heads]
    if counts is not None:
        s = [jnp.where(counts, s[j], -1e30) for j in heads]
    p = [jnp.exp2(s[j] - new[j]) for j in heads]
    update = [weigh(value(piece, j), p[j].astype(jnp.bfloat16)) for j in heads]
    shrink = [jnp.exp2(old[j][0] - new[j]) for j in heads]
    total = [old[j][1] * shrink[j] + jnp.sum(p[j], axis=0, keepdims=True) for j in heads]
    acc = [old[j][2] * shrink[j] + update[j] for j in heads]
    return list(zip(new, total, acc))


def finish(count, shift, slot, span_ref, q_ref, piece, *refs):
    refs = list(refs)
    top_in, total_in, acc_in = refs.pop(0), refs.pop(0), refs.pop(0)
    rows = piece.shape[0]
    if slot:
        refs.pop(0)
        out_ref, done, sems = refs
        before = span_ref[0:1, 0:1][0, 0] > 0.0
    else:
        out_ref, top_out, total_out, acc_out, flag, done, sems = refs
        (before,) = comes_before(count, [shift], span_ref)
        flag[...] = jnp.where(before, jnp.ones(flag.shape, jnp.float32), 0.0)

    def folded(i, counts):
        old = [(top_in[i, j], total_in[i, j], acc_in[i, j]) for j in range(KV_HEADS)]
        queries = [read_queries(q_ref, i, rows, j) for j in range(KV_HEADS)]
        return fold_heads(old, piece, queries, counts)

    def write(i, states):
        copies = []
        for j in range(KV_HEADS):
            _, total, acc = states[j]
            result = normalized(total, acc)
            for g in range(GROUP):
                h = j * GROUP + g
                done[i, :, h * HEAD_DIM : (h + 1) * HEAD_DIM] = result[g * rows : (g + 1) * rows]
            columns = slice(j * GROUP * HEAD_DIM, (j + 1) * GROUP * HEAD_DIM)
            copies.append(
                pltpu.make_async_copy(
                    done.at[i, :, columns], out_ref.at[i * rows : (i + 1) * rows, columns], sems.at[i, j]
                )
            )
            copies[-1].start()
        return copies

    if slot:

        @pl.when(jnp.logical_not(before))
        def _():
            for copy in write(1, folded(1, None)):
                copy.wait()

        return

    copies = write(0, folded(0, before))
    states = folded(1, None)
    for j in range(KV_HEADS):
        top_out[1, j], total_out[1, j], acc_out[1, j] = states[j]

    @pl.when(before)
    def _():
        kept = [(top_out[1, j], total_out[1, j], acc_out[1, j]) for j in range(KV_HEADS)]
        for copy in write(1, kept):
            copy.wait()

    for copy in copies:
        copy.wait()


def end(count, shift, slot, piece, state, out, span_ids, queries):
    tok_rows, features = queries.shape
    rows = tok_rows // 2
    vmem, hbm = pl.BlockSpec(memory_space=pltpu.VMEM), pl.BlockSpec(memory_space=pltpu.HBM)
    result = jax.ShapeDtypeStruct((tok_rows, features), queries.dtype)
    like = [jax.ShapeDtypeStruct(part.shape, part.dtype) for part in state]
    return pl.pallas_call(
        functools.partial(finish, count, shift, slot),
        out_shape=result if slot else [result, *like, jax.ShapeDtypeStruct((8, 128), jnp.float32)],
        in_specs=[vmem] * 6 + [hbm] * slot,
        out_specs=hbm if slot else [hbm] + [vmem] * 4,
        scratch_shapes=[
            pltpu.VMEM((2, rows, features), queries.dtype),
            pltpu.SemaphoreType.DMA((2, KV_HEADS)),
        ],
        input_output_aliases={6: 0} if slot else {},
        compiler_params=pltpu.CompilerParams(vmem_limit_bytes=32 * 1024 * 1024),
        cost_estimate=pl.CostEstimate(
            flops=2 * tok_rows * features * rows,
            bytes_accessed=4 * tok_rows * features,
            transcendentals=rows * tok_rows * KV_HEADS * GROUP // 2,
        ),
    )(span_ids, queries, piece, *state, *([out] if slot else []))


def fold(count, shifts, pieces, state, end, span_ids, queries):
    vmem = pl.BlockSpec(memory_space=pltpu.VMEM)
    tok_rows, features = queries.shape
    slot_rows = GROUP * (tok_rows // 2)
    begin = state is None
    state = [] if begin else list(state)
    if end:
        out_shape = jax.ShapeDtypeStruct((tok_rows, features), jnp.bfloat16)
    else:
        row = jax.ShapeDtypeStruct((2, KV_HEADS, 1, slot_rows), jnp.float32)
        out_shape = [row, row, jax.ShapeDtypeStruct((2, KV_HEADS, HEAD_DIM, slot_rows), jnp.float32)]
    keys = (len(pieces) // 2) * tok_rows
    return pl.pallas_call(
        functools.partial(attend, count, tuple(shifts), begin, end),
        out_shape=out_shape,
        in_specs=[vmem] * (2 + len(pieces) + len(state)),
        out_specs=vmem if end else [vmem] * 3,
        compiler_params=pltpu.CompilerParams(vmem_limit_bytes=32 * 1024 * 1024),
        cost_estimate=pl.CostEstimate(
            flops=2 * keys * features * tok_rows,
            bytes_accessed=2 * keys * 2 * WIDTH + 4 * tok_rows * features,
            transcendentals=keys * tok_rows * KV_HEADS * GROUP // 2,
        ),
    )(span_ids, queries, *pieces, *state)


def per_device(queries, keyvals, span_ids):
    count = lax.axis_size("ctx")
    rows = queries.shape[1] // 2
    order = ring_order(count)
    back = [(order[i], order[(i + 1) % count]) for i in range(count)]
    ahead = [(b, a) for a, b in back]

    flat = lax.optimization_barrier(keyvals[0].reshape(2 * rows, 2 * WIDTH))
    own = [flat[:rows], flat[rows:]]
    up, down = own, own
    last = count // 2
    held, state = ([], own), None
    for step in range(1, last + 1):
        if step > 1:
            state = fold(count, *held, state, False, span_ids, queries[0])
            if step == 2:
                up[0], *state = lax.optimization_barrier((up[0], *state))
            held = shifts, pieces
        if 2 * step < count:
            up = [lax.ppermute(piece, "ctx", ahead) for piece in up]
            down = [lax.ppermute(piece, "ctx", back) for piece in down]
            shifts, pieces = [step, -step], up + down
        else:
            shifts = [-step]
            pieces = [lax.ppermute(up[0], "ctx", ahead), lax.ppermute(down[1], "ctx", back)]
    if last:
        state = fold(count, *held, state, False, span_ids, queries[0])
        held = shifts, pieces
    if count % 2:
        return fold(count, *held, state, True, span_ids, queries[0])[None]
    out, *state, encloses = end(count, shifts[0], 0, pieces[0], state, None, span_ids, queries[0])
    return end(count, shifts[0], 1, pieces[1], state, out, encloses, queries[0])[None]


def solution(mesh):
    in_specs = (P("fsdp", "ctx", None), P("fsdp", "ctx", None, None), P("fsdp", None))
    out_specs = P("fsdp", "ctx", None)
    return jax.shard_map(
        per_device, mesh=mesh, in_specs=in_specs, out_specs=out_specs, check_vma=False
    )
```

```python
import functools
import math

import jax
import jax.numpy as jnp
from jax import lax
from jax.experimental import pallas as pl
from jax.experimental.pallas import tpu as pltpu
from jax.sharding import PartitionSpec as P

KV_HEADS = 4
GROUP = 4
HEAD_DIM = 128
WIDTH = KV_HEADS * HEAD_DIM
NT = (((1,), (1,)), ((), ()))
TN = (((0,), (0,)), ((), ()))


def ring_order(count):
    return [i for i in range(count) if i % 2 == 0] + [i for i in reversed(range(count)) if i % 2]


def ring_member(place, count):
    half = (count + 1) // 2
    return jnp.where(place < half, 2 * place, 2 * (count - 1 - place) + 1)


def ring_place(member, count):
    return jnp.where(member % 2 == 0, member // 2, count - 1 - member // 2)


def key(piece, j):
    return piece[:, j * HEAD_DIM : (j + 1) * HEAD_DIM]


def value(piece, j):
    return piece[:, WIDTH + j * HEAD_DIM : WIDTH + (j + 1) * HEAD_DIM]


def read_queries(q_ref, slot, rows, j):
    start = slot * rows if isinstance(slot, int) else pl.multiple_of(slot * rows, rows)
    return jnp.concatenate(
        [
            q_ref[pl.ds(start, rows), (j * GROUP + g) * HEAD_DIM : (j * GROUP + g + 1) * HEAD_DIM]
            for g in range(GROUP)
        ],
        axis=0,
    )


def scores(k, q):
    scale = math.log2(math.e) / math.sqrt(HEAD_DIM)
    return lax.dot_general(k, q, NT, preferred_element_type=jnp.float32) * scale


def weigh(v, p):
    return lax.dot_general(v, p, TN, preferred_element_type=jnp.float32)


def comes_before(count, shifts, span_ref):
    place = ring_place(lax.axis_index("ctx"), count)
    table = span_ref[...].astype(jnp.float32)
    lane = lax.broadcasted_iota(jnp.int32, table.shape, 1)

    def span_of(shift):
        member = ring_member((place + shift + count) % count, count)
        return jnp.sum(jnp.where(lane == 2 * member, table, 0.0))

    own_span = span_of(0)
    return [span_of(shift) < own_span for shift in shifts]


def normalized(total, acc):
    return (acc * (1.0 / total)).astype(jnp.bfloat16).T


def attend(count, shifts, begin, end, span_ref, q_ref, *refs):
    refs = list(refs)
    chunks = [(refs.pop(0), refs.pop(0)) for _ in range(len(shifts) + begin)]
    if not begin:
        top_in, total_in, acc_in = refs.pop(0), refs.pop(0), refs.pop(0)
    if end:
        out_ref = refs.pop(0)
    else:
        top_out, total_out, acc_out = refs
    rows = chunks[0][0].shape[0]
    slot_rows = GROUP * rows

    def queries(slot, j):
        return read_queries(q_ref, slot, rows, j)

    heads = range(KV_HEADS)
    result = {}
    if begin:
        early, late = chunks.pop(0)
        key_row = lax.broadcasted_iota(jnp.int32, (rows, slot_rows), 0)
        query_row = lax.broadcasted_iota(jnp.int32, (rows, slot_rows), 1) % rows
        causal = key_row <= query_row
        for j in heads:
            q = queries(0, j)
            s = jnp.where(causal, scores(key(early, j), q), -1e30)
            new = jnp.max(s, axis=0, keepdims=True)
            p = jnp.exp2(s - new)
            result[0, j] = new, jnp.sum(p, axis=0, keepdims=True), weigh(value(early, j), p.astype(jnp.bfloat16))
            q = queries(1, j)
            k = jnp.concatenate([key(early, j), key(late, j)], axis=0)
            v = jnp.concatenate([value(early, j), value(late, j)], axis=0)
            s = scores(k, q)
            s = jnp.concatenate([s[:rows], jnp.where(causal, s[rows:], -1e30)], axis=0)
            new = jnp.max(s, axis=0, keepdims=True)
            p = jnp.exp2(s - new)
            result[1, j] = new, jnp.sum(p, axis=0, keepdims=True), weigh(v, p.astype(jnp.bfloat16))
    else:
        n = len(shifts)
        befores = comes_before(count, shifts, span_ref)
        slots = [jnp.where(before, 0, 1) for before in befores]
        picked = [
            jnp.where(before, early[...], late[...]) for before, (early, late) in zip(befores, chunks)
        ]
        full, part = {}, {}
        for j in heads:
            k = jnp.concatenate([key(early, j) for early, _ in chunks], axis=0)
            full[j] = scores(k, queries(1, j))
            part[j] = [scores(key(picked[i], j), queries(slots[i], j)) for i in range(n)]
        for j in heads:
            old = [top_in[0, j], top_in[1, j]]
            most = [jnp.max(s, axis=0, keepdims=True) for s in part[j]]
            new = [old[0], jnp.maximum(old[1], jnp.max(full[j], axis=0, keepdims=True))]
            for i in range(n):
                new[0] = jnp.maximum(new[0], jnp.where(befores[i], most[i], -1e30))
                new[1] = jnp.maximum(new[1], jnp.where(befores[i], -1e30, most[i]))
            p = jnp.exp2(full[j] - new[1])
            shrink = [jnp.exp2(old[slot] - new[slot]) for slot in range(2)]
            added = [total_in[0, j] * shrink[0], total_in[1, j] * shrink[1] + jnp.sum(p, axis=0, keepdims=True)]
            weights = [[], [p.astype(jnp.bfloat16)]]
            values = [[value(picked[i], j) for i in range(n)], [value(early, j) for early, _ in chunks]]
            values[1] += values[0]
            for i in range(n):
                p = jnp.exp2(part[j][i] - jnp.where(befores[i], new[0], new[1]))
                t = jnp.sum(p, axis=0, keepdims=True)
                p = p.astype(jnp.bfloat16)
                zero = jnp.zeros_like(p)
                added[0] = added[0] + jnp.where(befores[i], t, 0.0)
                added[1] = added[1] + jnp.where(befores[i], 0.0, t)
                weights[0].append(jnp.where(befores[i], p, zero))
                weights[1].append(jnp.where(befores[i], zero, p))
            for slot in range(2):
                update = weigh(
                    jnp.concatenate(values[slot], axis=0), jnp.concatenate(weights[slot], axis=0)
                )
                result[slot, j] = new[slot], added[slot], acc_in[slot, j] * shrink[slot] + update

    for (slot, j), (new, added, update) in result.items():
        if end:
            done = normalized(added, update)
            for g in range(GROUP):
                h = j * GROUP + g
                out_ref[
                    slot * rows : (slot + 1) * rows, h * HEAD_DIM : (h + 1) * HEAD_DIM
                ] = done[g * rows : (g + 1) * rows]
        else:
            top_out[slot, j] = new
            total_out[slot, j] = added
            acc_out[slot, j] = update


def fold_heads(old, piece, queries, counts):
    heads = range(KV_HEADS)
    s = [scores(key(piece, j), queries[j]) for j in heads]
    most = [jnp.max(s[j], axis=0, keepdims=True) for j in heads]
    if counts is not None:
        most = [jnp.where(counts, most[j], -1e30) for j in heads]
    new = [jnp.maximum(old[j][0], most[j]) for j in heads]
    if counts is not None:
        s = [jnp.where(counts, s[j], -1e30) for j in heads]
    p = [jnp.exp2(s[j] - new[j]) for j in heads]
    update = [weigh(value(piece, j), p[j].astype(jnp.bfloat16)) for j in heads]
    shrink = [jnp.exp2(old[j][0] - new[j]) for j in heads]
    total = [old[j][1] * shrink[j] + jnp.sum(p[j], axis=0, keepdims=True) for j in heads]
    acc = [old[j][2] * shrink[j] + update[j] for j in heads]
    return list(zip(new, total, acc))


def finish(count, shift, slot, span_ref, q_ref, piece, *refs):
    refs = list(refs)
    top_in, total_in, acc_in = refs.pop(0), refs.pop(0), refs.pop(0)
    rows = piece.shape[0]
    if slot:
        refs.pop(0)
        out_ref, done, sems = refs
        before = span_ref[0:1, 0:1][0, 0] > 0.0
    else:
        out_ref, top_out, total_out, acc_out, flag, done, sems = refs
        (before,) = comes_before(count, [shift], span_ref)
        flag[...] = jnp.where(before, jnp.ones(flag.shape, jnp.float32), 0.0)

    def folded(i, counts):
        old = [(top_in[i, j], total_in[i, j], acc_in[i, j]) for j in range(KV_HEADS)]
        queries = [read_queries(q_ref, i, rows, j) for j in range(KV_HEADS)]
        return fold_heads(old, piece, queries, counts)

    def write(i, states):
        copies = []
        for j in range(KV_HEADS):
            _, total, acc = states[j]
            result = normalized(total, acc)
            for g in range(GROUP):
                h = j * GROUP + g
                done[i, :, h * HEAD_DIM : (h + 1) * HEAD_DIM] = result[g * rows : (g + 1) * rows]
            columns = slice(j * GROUP * HEAD_DIM, (j + 1) * GROUP * HEAD_DIM)
            copies.append(
                pltpu.make_async_copy(
                    done.at[i, :, columns], out_ref.at[i * rows : (i + 1) * rows, columns], sems.at[i, j]
                )
            )
            copies[-1].start()
        return copies

    if slot:

        @pl.when(jnp.logical_not(before))
        def _():
            for copy in write(1, folded(1, None)):
                copy.wait()

        return

    copies = write(0, folded(0, before))
    states = folded(1, None)
    for j in range(KV_HEADS):
        top_out[1, j], total_out[1, j], acc_out[1, j] = states[j]

    @pl.when(before)
    def _():
        kept = [(top_out[1, j], total_out[1, j], acc_out[1, j]) for j in range(KV_HEADS)]
        for copy in write(1, kept):
            copy.wait()

    for copy in copies:
        copy.wait()


def end(count, shift, slot, piece, state, out, span_ids, queries):
    tok_rows, features = queries.shape
    rows = tok_rows // 2
    vmem, hbm = pl.BlockSpec(memory_space=pltpu.VMEM), pl.BlockSpec(memory_space=pltpu.HBM)
    result = jax.ShapeDtypeStruct((tok_rows, features), queries.dtype)
    like = [jax.ShapeDtypeStruct(part.shape, part.dtype) for part in state]
    return pl.pallas_call(
        functools.partial(finish, count, shift, slot),
        out_shape=result if slot else [result, *like, jax.ShapeDtypeStruct((8, 128), jnp.float32)],
        in_specs=[vmem] * 6 + [hbm] * slot,
        out_specs=hbm if slot else [hbm] + [vmem] * 4,
        scratch_shapes=[
            pltpu.VMEM((2, rows, features), queries.dtype),
            pltpu.SemaphoreType.DMA((2, KV_HEADS)),
        ],
        input_output_aliases={6: 0} if slot else {},
        compiler_params=pltpu.CompilerParams(vmem_limit_bytes=32 * 1024 * 1024),
        cost_estimate=pl.CostEstimate(
            flops=2 * tok_rows * features * rows,
            bytes_accessed=4 * tok_rows * features,
            transcendentals=rows * tok_rows * KV_HEADS * GROUP // 2,
        ),
    )(span_ids, queries, piece, *state, *([out] if slot else []))


def fold(count, shifts, pieces, state, end, span_ids, queries):
    vmem = pl.BlockSpec(memory_space=pltpu.VMEM)
    tok_rows, features = queries.shape
    slot_rows = GROUP * (tok_rows // 2)
    begin = state is None
    state = [] if begin else list(state)
    if end:
        out_shape = jax.ShapeDtypeStruct((tok_rows, features), jnp.bfloat16)
    else:
        row = jax.ShapeDtypeStruct((2, KV_HEADS, 1, slot_rows), jnp.float32)
        out_shape = [row, row, jax.ShapeDtypeStruct((2, KV_HEADS, HEAD_DIM, slot_rows), jnp.float32)]
    keys = (len(pieces) // 2) * tok_rows
    return pl.pallas_call(
        functools.partial(attend, count, tuple(shifts), begin, end),
        out_shape=out_shape,
        in_specs=[vmem] * (2 + len(pieces) + len(state)),
        out_specs=vmem if end else [vmem] * 3,
        compiler_params=pltpu.CompilerParams(vmem_limit_bytes=32 * 1024 * 1024),
        cost_estimate=pl.CostEstimate(
            flops=2 * keys * features * tok_rows,
            bytes_accessed=2 * keys * 2 * WIDTH + 4 * tok_rows * features,
            transcendentals=keys * tok_rows * KV_HEADS * GROUP // 2,
        ),
    )(span_ids, queries, *pieces, *state)


def per_device(queries, keyvals, span_ids):
    count = lax.axis_size("ctx")
    rows = queries.shape[1] // 2
    order = ring_order(count)
    ahead = [(order[i], order[(i + 1) % count]) for i in range(count)]
    back = [(b, a) for a, b in ahead]

    flat = lax.optimization_barrier(keyvals[0].reshape(2 * rows, 2 * WIDTH))
    own = [flat[:rows], flat[rows:]]
    up, down = own, own
    last = count // 2
    held, state = ([], own), None
    for step in range(1, last + 1):
        if step > 1:
            if step % 2 == 0:
                state = fold(count, *held, state, False, span_ids, queries[0])
                held = [], []
            if step == 2:
                up[0], *state = lax.optimization_barrier((up[0], *state))
            held = held[0] + shifts, held[1] + pieces
        if 2 * step < count:
            up = [lax.ppermute(piece, "ctx", ahead) for piece in up]
            down = [lax.ppermute(piece, "ctx", back) for piece in down]
            shifts, pieces = [-step, step], up + down
        else:
            shifts = [-step]
            pieces = [lax.ppermute(up[0], "ctx", ahead), lax.ppermute(down[1], "ctx", back)]
    if last:
        state = fold(count, *held, state, False, span_ids, queries[0])
        held = shifts, pieces
    if count % 2:
        return fold(count, *held, state, True, span_ids, queries[0])[None]
    out, *state, encloses = end(count, shifts[0], 0, pieces[0], state, None, span_ids, queries[0])
    return end(count, shifts[0], 1, pieces[1], state, out, encloses, queries[0])[None]


def solution(mesh):
    in_specs = (P("fsdp", "ctx", None), P("fsdp", "ctx", None, None), P("fsdp", None))
    out_specs = P("fsdp", "ctx", None)
    return jax.shard_map(
        per_device, mesh=mesh, in_specs=in_specs, out_specs=out_specs, check_vma=False
    )
```
